256 devices in a mesh: dp: 16 (over x_lo, y, core), tensor: 16 (over z, x_hi).
Axes of the slice: x: 4 (x_hi: 2, x_lo: 2; x = x_hi * 2 + x_lo), y: 4, z: 8, core: 2. Of those that a mesh axis runs over, the one named last changes fastest.
Arguments:
- tokens: bfloat16 [2048, 32768], P('dp', 'tensor'), may hold values from -6 to 6
- factors: bfloat16 [8, 256, 2, 128, 128], P(None, 'tensor'), may hold values from -0.375 to 0.375
- cotangent: bfloat16 [2048, 32768], P('dp', 'tensor'), may hold values from -6 to 6
Outputs:
- mixed: bfloat16 [2048, 32768], P('dp', 'tensor')
- token_grad: bfloat16 [2048, 32768], P('dp', 'tensor')
- factor_grad: float32 [8, 256, 2, 128, 128], P(None, 'tensor', None, 'dp')
The draws below stay inside these ranges and needn't reach their ends.
All inputs are finite; a program needn't handle non-finite values.
Results may differ from the reference program's by a relative error of at most 0.017.
Values may be sent and summed in bfloat16 or wider, within the bound.
A program may use at most 128 MiB of HBM per device.

```python
import jax
import jax.numpy as jnp
from jax import lax

LEVELS = 8
BS = 128
NBLK = 256
ORDER = 32768
TOKENS = 2048


def levels(key, shape, pieces, least, top_value):
    def one(position, shards_of):
        steps = jax.random.uniform(jax.random.fold_in(jax.random.fold_in(key, 6), position), (shards_of,), jnp.float32, least / len(pieces), top_value / len(pieces))
        return jnp.repeat(jnp.exp(steps), shape[position] // shards_of).reshape((-1,) + (1,) * (len(shape) - position - 1))

    factor_of = one(*pieces[0])
    for cut in pieces[1:]:
        factor_of = factor_of * one(*cut)
    return factor_of


def bell_draw(stream_key, extent, scale, reach, shards=(), held_as=jnp.bfloat16):
    array = scale * jax.random.normal(stream_key, extent, jnp.float32)
    if shards:
        array = array * levels(stream_key, extent, shards, -0.22, 0.18)
    return jnp.clip(array, -reach, reach).astype(held_as)


def setup_inputs(seed: int = 0) -> dict:
    splits = jax.random.split(jax.random.key(seed), 4)
    tokens = bell_draw(splits[0], (TOKENS, ORDER), 1.0, 6.0, ((0, 16), (1, 16)))
    factors = bell_draw(splits[1], (LEVELS, NBLK, 2, BS, BS), (2 * BS) ** -0.5, 0.375, ((1, 16),))
    cotangent = bell_draw(splits[2], (TOKENS, ORDER), 1.0, 6.0, ((0, 16), (1, 16)))
    return dict(tokens=tokens, factors=factors, cotangent=cotangent)


def pair_flip(x, dist):
    t, b, f = x.shape
    r = x.reshape(t, b // (2 * dist), 2, dist, f)
    return jnp.flip(r, 2).reshape(t, b, f)


def reference(tokens, factors, cotangent):
    rows = tokens.shape[0]
    x = tokens.reshape(rows, NBLK, BS)
    saved = []
    for level in range(LEVELS):
        weight = factors[level].astype(jnp.float32)
        partner = pair_flip(x, 2 ** level)
        saved.append((x, partner))
        stacked = jnp.stack([x, partner], 2).astype(jnp.float32)
        x = jnp.einsum('tbki,bkio->tbo', stacked, weight).astype(jnp.bfloat16)
    mixed = x.reshape(rows, ORDER)
    grad = cotangent.reshape(rows, NBLK, BS)
    grads = [None] * LEVELS
    for level in reversed(range(LEVELS)):
        weight = factors[level].astype(jnp.float32)
        g32 = grad.astype(jnp.float32)
        own = jnp.einsum('tbo,bio->tbi', g32, weight[:, 0])
        cross = jnp.einsum('tbo,bio->tbi', g32, weight[:, 1]).astype(jnp.bfloat16)
        cross = lax.optimization_barrier(pair_flip(cross, 2 ** level))
        xin, partner = saved[level]
        stacked = jnp.stack([xin, partner], 2).astype(jnp.float32)
        grads[level] = jnp.einsum('tbki,tbo->bkio', stacked, g32)
        grad = (own + cross.astype(jnp.float32)).astype(jnp.bfloat16)
    token_grad = grad.reshape(rows, ORDER)
    return mixed, token_grad, jnp.stack(grads, 0)
```

```python
import jax
import jax.numpy as jnp
from jax import lax
from jax.experimental import pallas as pl
from jax.experimental.pallas import tpu as pltpu
from jax.sharding import PartitionSpec as P

MESH = pl.DeviceIdType.MESH
BF = jnp.bfloat16
F32 = jnp.float32

S_X0, S_W, S_FZ, S_CA, S_XA, S_GA, S_MA, S_HA, S_TG, S_OB = range(10)
S_AG, S_CF, S_CD, S_RS, S_FS, N_SEM = 10, 14, 18, 26, 34, 42


def pair(q, d):
    return (q // d) * (2 * d) + q % d


def wide(a, b):
    return jnp.concatenate([a, b], axis=1)


def kernel(
    tok, fac, cot, mixed, tgrad, fgrad,
    xo, xt, go, gt, w, wt, csend, crecv, part, got, acc, fin, hs, hr, ob,
    rsem, ssem,
):
    dp, t = lax.axis_index("dp"), lax.axis_index("tensor")
    c, s = dp % 2, dp // 2
    oc = 1 - c
    xl, y = s // 4, s % 4

    def far(k):
        return (t + 8 + ((k + 1) // 2) * (1 - 2 * (k % 2))) % 16

    def chip(i):
        return ((xl + i // 4) % 2) * 4 + (y + i % 4) % 4

    def send(src, dst, slot, device):
        pltpu.make_async_remote_copy(
            src_ref=src, dst_ref=dst, send_sem=ssem.at[slot], recv_sem=rsem.at[slot],
            device_id=device, device_id_type=MESH,
        ).start()

    def local(src, dst, slot):
        pltpu.make_async_copy(src, dst, rsem.at[slot]).start()

    def arrived(ref, slot):
        pltpu.make_async_copy(ref, ref, rsem.at[slot]).wait()

    def left(ref, slot):
        pltpu.make_async_copy(ref, ref, ssem.at[slot]).wait()

    def loop(n, body, unroll=1):
        def step(i, carry):
            body(i)
            return carry

        lax.fori_loop(0, n, step, 0, unroll=unroll)

    sibling = (s * 2 + oc, t)

    def to_tensor(src, dst, slot):
        loop(15, lambda k: send(src(far(k)), dst, slot, (dp, far(k))))
        local(src(t), dst, slot)

    def to_chips(src, dst, slot):
        loop(7, lambda k: send(src(chip(k + 1)), dst, slot, (chip(k + 1) * 2 + c, t)))

    loop(16, lambda j: local(tok.at[:, pl.ds(pl.multiple_of(j * 128, 128), 128)], xo.at[0, j], S_X0))
    local(fac.at[pl.ds(0, 4)], w, S_W)

    barrier = pltpu.get_barrier_semaphore()

    def greet(device):
        pl.semaphore_signal(barrier, inc=1, device_id=device, device_id_type=MESH)

    loop(15, lambda k: greet((dp, far(k))))
    loop(7, lambda k: greet((chip(k + 1) * 2 + c, t)))
    greet(sibling)
    pl.semaphore_wait(barrier, 23)

    rows = pl.ds(pl.multiple_of(s * 16, 16), 16)
    to_tensor(lambda j: fac.at[pl.ds(4, 4), j, c, rows, :], wt.at[:, c, s, t], S_FZ)
    to_tensor(
        lambda j: cot.at[:, pl.ds(pl.multiple_of(j * 128, 128), 128)], gt.at[4, t], S_CA
    )

    def weights_low(level):
        return lambda b, k: w[level, b, k]

    def weights_high(lv):
        return lambda b, k: wt[lv, k, :, b].reshape(128, 128)

    def matrix(weights, b0, b1):
        return jnp.concatenate(
            [wide(weights(b0, 0), weights(b1, 1)), wide(weights(b0, 1), weights(b1, 0))], axis=0
        )

    def forward(x, at, d, weights):
        def body(q):
            b0 = pair(q, d)
            b1 = b0 + d
            new = jnp.dot(
                wide(x[at, b0], x[at, b1]), matrix(weights, b0, b1), preferred_element_type=F32
            ).astype(BF)
            x[at + 1, b0] = new[:, :128]
            x[at + 1, b1] = new[:, 128:]

        loop(8, body, 2)

    def backward(g, at, d, weights):
        def body(q):
            b0 = pair(q, d)
            b1 = b0 + d
            new = lax.dot_general(
                wide(g[at + 1, b0], g[at + 1, b1]), matrix(weights, b0, b1),
                (((1,), (1,)), ((), ())), preferred_element_type=F32,
            ).astype(BF)
            g[at, b0] = new[:, :128]
            g[at, b1] = new[:, 128:]

        loop(8, body, 2)

    def gradient(x, g, at, d, core, put):
        dl = min(d, 4)

        def body(q):
            b0 = pair(core * 4 + q, d)
            b1 = b0 + d
            dm = lax.dot_general(
                wide(x[at, b0], x[at, b1]), wide(g[at + 1, b0], g[at + 1, b1]),
                (((0,), (0,)), ((), ())), preferred_element_type=F32,
            )
            m0 = pair(q, dl)
            m1 = m0 + dl
            put(m0, 0, dm[:128, :128].reshape(8, 16, 128))
            put(m0, 1, dm[128:, :128].reshape(8, 16, 128))
            put(m1, 1, dm[:128, 128:].reshape(8, 16, 128))
            put(m1, 0, dm[128:, 128:].reshape(8, 16, 128))

        loop(4, body, 2)

    def side(level):
        return (xo, go, level) if level < 4 else (xt, gt, level - 4)

    def grad_out(level):
        x, g, at = side(level)

        def put(m, k, value):
            csend[level, :, m, k] = value.astype(BF)

        gradient(x, g, at, 2**at, oc, put)
        send(csend.at[level], crecv.at[level], S_CD + level, sibling)

    def grad_in(level):
        x, g, at = side(level)
        arrived(crecv.at[level], S_CD + level)

        def put(m, k, value):
            part[level, :, m, k] = (value + crecv[level, :, m, k].astype(F32)).astype(BF)

        gradient(x, g, at, 2**at, c, put)
        to_chips(lambda i: part.at[level, i], got.at[level, s], S_RS + level)
        local(part.at[level, s], got.at[level, s], S_RS + level)

    def finish(level, out, at):
        arrived(got.at[level], S_RS + level)

        def body(m):
            total = got[level, 0, m].astype(F32)
            for i in range(1, 8):
                total = total + got[level, i, m].astype(F32)
            acc[level, m] = total

        loop(8, body, 2)
        for u in range(2):
            first = 8 * c + 4 * u if level % 4 < 3 else 8 * u + 4 * c
            dst = out.at[at, pl.ds(first, 4)]
            mine = pl.ds(pl.multiple_of(c * 8, 8), 8)
            other = pl.ds(pl.multiple_of(oc * 8, 8), 8)
            local(acc.at[level, pl.ds(4 * u, 4), :, mine], dst, S_FS + level)
            send(acc.at[level, pl.ds(4 * u, 4), :, other], dst, S_FS + level, sibling)

    arrived(xo.at[0], S_X0)
    arrived(w, S_W)
    for level in range(4):
        forward(xo, level, 2**level, weights_low(level))
    to_tensor(lambda j: xo.at[4, j], xt.at[0, t], S_XA)

    arrived(wt.at[:, c, s], S_FZ)
    for lv in (3, 2, 1, 0):
        to_chips(lambda i, lv=lv: wt.at[lv, c, s], wt.at[lv, c, s], S_AG + lv)

    def pass_on(lv):
        arrived(wt.at[lv, c, pl.ds(0, 7)], S_AG + lv)
        send(wt.at[lv, c], wt.at[lv, c], S_CF + lv, sibling)

    pass_on(3)
    arrived(gt.at[4], S_CA)
    for lv in (3, 2, 1, 0):
        if lv > 0:
            pass_on(lv - 1)
        arrived(wt.at[lv, oc], S_CF + lv)
        backward(gt, lv, 2**lv, weights_high(lv))
    to_tensor(lambda j: gt.at[0, j], go.at[4, t], S_GA)

    arrived(xt.at[0], S_XA)
    for level in range(4, 8):
        grad_out(level)
        forward(xt, level - 4, 2 ** (level - 4), weights_high(level - 4))
        if level > 4:
            grad_in(level - 1)
    to_tensor(lambda j: xt.at[4, j], mixed.at[:, pl.ds(pl.multiple_of(t * 128, 128), 128)], S_MA)
    grad_in(7)

    arrived(go.at[4], S_GA)
    for level in (3, 2, 1, 0):
        grad_out(level)
        backward(go, level, 2**level, weights_low(level))
        if level < 3:
            grad_in(level + 1)
    loop(16, lambda j: local(go.at[0, j], tgrad.at[:, pl.ds(pl.multiple_of(j * 128, 128), 128)], S_TG))
    grad_in(0)

    for level in range(4, 8):
        finish(level, fin, level - 4)
    for level in range(4, 8):
        arrived(fin.at[level - 4], S_FS + level)

    def pack(h):
        for lv in range(4):
            hs[h, lv] = fin[lv, h].reshape(16, 128).astype(BF)

    loop(16, pack)
    to_tensor(lambda j: hs.at[j], hr.at[t], S_HA)

    for level in (3, 2, 1, 0):
        finish(level, fgrad, level)

    arrived(hr, S_HA)

    def unpack(j):
        for lv in range(4):
            ob[lv, j] = hr[j, lv].astype(F32).reshape(2, 8, 128)

    loop(16, unpack)
    local(ob, fgrad.at[pl.ds(4, 4)], S_OB)

    for level in range(4):
        arrived(fgrad.at[level], S_FS + level)
    arrived(mixed, S_MA)
    arrived(tgrad, S_TG)
    arrived(fgrad.at[pl.ds(4, 4)], S_OB)
    blocks = xo.at[0, pl.ds(0, 15)]
    for slot in (S_CA, S_XA, S_GA, S_MA):
        left(blocks, slot)
    left(hs.at[pl.ds(0, 15)], S_FZ)
    left(hs.at[pl.ds(0, 15)], S_HA)
    for lv in range(4):
        left(wt.at[lv, 0, pl.ds(0, 7)], S_AG + lv)
        left(wt.at[lv, 0], S_CF + lv)
    for level in range(8):
        left(csend.at[level], S_CD + level)
        left(part.at[level, pl.ds(0, 7)], S_RS + level)
        left(acc.at[level, :, :, pl.ds(0, 8)], S_FS + level)


def per_device(tokens, factors, cotangent):
    hbm = pl.BlockSpec(memory_space=pl.ANY)
    acts = pltpu.VMEM((5, 16, 128, 128), BF)
    grads = pltpu.VMEM((8, 8, 8, 2, 16, 128), BF)
    return pl.pallas_call(
        kernel,
        out_shape=(
            jax.ShapeDtypeStruct((128, 2048), BF),
            jax.ShapeDtypeStruct((128, 2048), BF),
            jax.ShapeDtypeStruct((8, 16, 2, 8, 128), F32),
        ),
        in_specs=[hbm] * 3,
        out_specs=[hbm] * 3,
        scratch_shapes=[
            acts, acts, acts, acts,
            pltpu.VMEM((4, 16, 2, 128, 128), BF),
            pltpu.VMEM((4, 2, 8, 16, 16, 128), BF),
            grads, grads, grads, grads,
            pltpu.VMEM((8, 8, 2, 16, 128), F32),
            pltpu.VMEM((4, 16, 2, 8, 128), F32),
            pltpu.VMEM((16, 4, 16, 128), BF),
            pltpu.VMEM((16, 4, 16, 128), BF),
            pltpu.VMEM((4, 16, 2, 8, 128), F32),
            pltpu.SemaphoreType.DMA((N_SEM,)),
            pltpu.SemaphoreType.DMA((N_SEM,)),
        ],
        compiler_params=pltpu.CompilerParams(
            collective_id=0, has_side_effects=True, vmem_limit_bytes=56 * 1024 * 1024
        ),
        cost_estimate=pl.CostEstimate(flops=3221225472, bytes_accessed=12582912, transcendentals=0),
        name="butterfly",
    )(tokens, factors, cotangent)


def solution(mesh):
    placed = (P("dp", "tensor"), P(None, "tensor", None, None, None), P("dp", "tensor"))
    return jax.shard_map(
        per_device,
        mesh=mesh,
        in_specs=placed,
        out_specs=(P("dp", "tensor"), P("dp", "tensor"), P(None, "tensor", None, "dp", None)),
        check_vma=False,
    )
```

```python
import jax
import jax.numpy as jnp
from jax import lax
from jax.experimental import pallas as pl
from jax.experimental.pallas import tpu as pltpu
from jax.sharding import PartitionSpec as P

MESH = pl.DeviceIdType.MESH
BF = jnp.bfloat16
F32 = jnp.float32

S_X0, S_W, S_FZ, S_CA, S_XA, S_GA, S_MA, S_HA, S_TG, S_OB = range(10)
S_AX, S_AY, S_CF, S_CD, S_RY, S_RX, S_FS, N_SEM = 10, 14, 18, 22, 30, 38, 46, 54


def pair(q, d):
    return (q // d) * (2 * d) + q % d


def wide(a, b):
    return jnp.concatenate([a, b], axis=1)


def kernel(
    tok, fac, cot, mixed, tgrad, fgrad,
    xo, xt, go, gt, w, wt, csend, crecv, part, got, mid, other, acc, fin, hs, hr, ob,
    rsem, ssem,
):
    dp, t = lax.axis_index("dp"), lax.axis_index("tensor")
    c, s = dp % 2, dp // 2
    oc = 1 - c
    xl, y = s // 4, s % 4

    def far(k):
        return (t + 8 + ((k + 1) // 2) * (1 - 2 * (k % 2))) % 16

    def along(i):
        return (y + i) % 4

    def send(src, dst, slot, device):
        pltpu.make_async_remote_copy(
            src_ref=src, dst_ref=dst, send_sem=ssem.at[slot], recv_sem=rsem.at[slot],
            device_id=device, device_id_type=MESH,
        ).start()

    def local(src, dst, slot):
        pltpu.make_async_copy(src, dst, rsem.at[slot]).start()

    def arrived(ref, slot):
        pltpu.make_async_copy(ref, ref, rsem.at[slot]).wait()

    def left(ref, slot):
        pltpu.make_async_copy(ref, ref, ssem.at[slot]).wait()

    def loop(n, body, unroll=1):
        def step(i, carry):
            body(i)
            return carry

        lax.fori_loop(0, n, step, 0, unroll=unroll)

    sibling = (s * 2 + oc, t)
    across = ((s + 4) % 8 * 2 + c, t)

    def to_tensor(src, dst, slot):
        loop(15, lambda k: send(src(far(k)), dst, slot, (dp, far(k))))
        local(src(t), dst, slot)

    def to_row(src, dst, slot):
        for i in (2, 1, 3):
            send(src(along(i)), dst, slot, ((xl * 4 + along(i)) * 2 + c, t))

    loop(16, lambda j: local(tok.at[:, pl.ds(pl.multiple_of(j * 128, 128), 128)], xo.at[0, j], S_X0))
    local(fac.at[pl.ds(0, 4)], w, S_W)

    barrier = pltpu.get_barrier_semaphore()

    def greet(device):
        pl.semaphore_signal(barrier, inc=1, device_id=device, device_id_type=MESH)

    loop(15, lambda k: greet((dp, far(k))))
    for i in (1, 2, 3):
        greet(((xl * 4 + along(i)) * 2 + c, t))
    greet(across)
    greet(sibling)
    pl.semaphore_wait(barrier, 20)

    rows = pl.ds(pl.multiple_of(s * 16, 16), 16)
    to_tensor(lambda j: fac.at[pl.ds(4, 4), j, c, rows, :], wt.at[:, c, xl, y, t], S_FZ)
    to_tensor(
        lambda j: cot.at[:, pl.ds(pl.multiple_of(j * 128, 128), 128)], gt.at[4, t], S_CA
    )

    def weights_low(level):
        return lambda b, k: w[level, b, k]

    def weights_high(lv):
        return lambda b, k: wt[lv, k, :, :, b].reshape(128, 128)

    def matrix(weights, b0, b1):
        return jnp.concatenate(
            [wide(weights(b0, 0), weights(b1, 1)), wide(weights(b0, 1), weights(b1, 0))], axis=0
        )

    def forward(x, at, d, weights):
        def body(q):
            b0 = pair(q, d)
            b1 = b0 + d
            new = jnp.dot(
                wide(x[at, b0], x[at, b1]), matrix(weights, b0, b1), preferred_element_type=F32
            ).astype(BF)
            x[at + 1, b0] = new[:, :128]
            x[at + 1, b1] = new[:, 128:]

        loop(8, body, 8)

    def backward(g, at, d, weights):
        def body(q):
            b0 = pair(q, d)
            b1 = b0 + d
            new = lax.dot_general(
                wide(g[at + 1, b0], g[at + 1, b1]), matrix(weights, b0, b1),
                (((1,), (1,)), ((), ())), preferred_element_type=F32,
            ).astype(BF)
            g[at, b0] = new[:, :128]
            g[at, b1] = new[:, 128:]

        loop(8, body, 8)

    def gradient(x, g, at, d, core, put):
        dl = min(d, 4)

        def body(q):
            b0 = pair(core * 4 + q, d)
            b1 = b0 + d
            dm = lax.dot_general(
                wide(x[at, b0], x[at, b1]), wide(g[at + 1, b0], g[at + 1, b1]),
                (((0,), (0,)), ((), ())), preferred_element_type=F32,
            )
            m0 = pair(q, dl)
            m1 = m0 + dl
            put(m0, 0, dm[:128, :128].reshape(2, 4, 16, 128))
            put(m0, 1, dm[128:, :128].reshape(2, 4, 16, 128))
            put(m1, 1, dm[:128, 128:].reshape(2, 4, 16, 128))
            put(m1, 0, dm[128:, 128:].reshape(2, 4, 16, 128))

        loop(4, body, 4)

    def side(level):
        return (xo, go, level) if level < 4 else (xt, gt, level - 4)

    def grad_out(level):
        x, g, at = side(level)

        def put(m, k, value):
            csend[level, :, :, m, k] = value.astype(BF)

        gradient(x, g, at, 2**at, oc, put)
        send(csend.at[level], crecv.at[level], S_CD + level, sibling)

    def grad_in(level):
        x, g, at = side(level)
        arrived(crecv.at[level], S_CD + level)

        def put(m, k, value):
            part[level, :, :, m, k] = (value + crecv[level, :, :, m, k].astype(F32)).astype(BF)

        gradient(x, g, at, 2**at, c, put)
        to_row(lambda i: part.at[level, :, i], got.at[level, :, y], S_RY + level)

    def gather(level):
        arrived(got.at[level, :, pl.ds(0, 3)], S_RY + level)

        def total(side_of, m):
            value = part[level, side_of, y, m].astype(F32)
            for i in (1, 2, 3):
                value = value + got[level, side_of, along(i), m].astype(F32)
            return value

        def give(m):
            mid[level, m] = total(1 - xl, m).astype(BF)

        def keep(m):
            acc[level, m] = total(xl, m)

        loop(8, give, 4)
        send(mid.at[level], other.at[level], S_RX + level, across)
        loop(8, keep, 4)

    def finish(level, out, at):
        arrived(other.at[level], S_RX + level)

        def body(m):
            acc[level, m] = acc[level, m] + other[level, m].astype(F32)

        loop(8, body, 4)
        for u in range(2):
            first = 8 * c + 4 * u if level % 4 < 3 else 8 * u + 4 * c
            dst = out.at[at, pl.ds(first, 4)]
            mine = pl.ds(pl.multiple_of(c * 8, 8), 8)
            theirs = pl.ds(pl.multiple_of(oc * 8, 8), 8)
            local(acc.at[level, pl.ds(4 * u, 4), :, mine], dst, S_FS + level)
            send(acc.at[level, pl.ds(4 * u, 4), :, theirs], dst, S_FS + level, sibling)

    arrived(xo.at[0], S_X0)
    arrived(w, S_W)
    for level in range(4):
        forward(xo, level, 2**level, weights_low(level))

    arrived(wt.at[:, c, xl, y], S_FZ)
    for lv in (3, 2, 1, 0):
        piece = wt.at[lv, c, xl, y]
        send(piece, piece, S_AX + lv, across)
        to_row(lambda i, piece=piece: piece, piece, S_AY + lv)
    for lv in (3, 2, 1, 0):
        piece = wt.at[lv, c, 1 - xl, y]
        arrived(piece, S_AX + lv)
        to_row(lambda i, piece=piece: piece, piece, S_AY + lv)

    def pass_on(lv):
        arrived(wt.at[lv, c, :, pl.ds(0, 3)], S_AY + lv)
        send(wt.at[lv, c], wt.at[lv, c], S_CF + lv, sibling)

    pass_on(3)
    arrived(gt.at[4], S_CA)
    to_tensor(lambda j: xo.at[4, j], xt.at[0, t], S_XA)
    for lv in (3, 2, 1, 0):
        if lv > 0:
            pass_on(lv - 1)
        arrived(wt.at[lv, oc], S_CF + lv)
        backward(gt, lv, 2**lv, weights_high(lv))
    to_tensor(lambda j: gt.at[0, j], go.at[4, t], S_GA)

    arrived(xt.at[0], S_XA)
    for level in range(4, 8):
        grad_out(level)
        forward(xt, level - 4, 2 ** (level - 4), weights_high(level - 4))
        if level > 4:
            grad_in(level - 1)
    to_tensor(lambda j: xt.at[4, j], mixed.at[:, pl.ds(pl.multiple_of(t * 128, 128), 128)], S_MA)
    grad_in(7)

    gather(4)

    arrived(go.at[4], S_GA)
    for level in (3, 2, 1, 0):
        grad_out(level)
        backward(go, level, 2**level, weights_low(level))
        if level < 3:
            grad_in(level + 1)
    loop(16, lambda j: local(go.at[0, j], tgrad.at[:, pl.ds(pl.multiple_of(j * 128, 128), 128)], S_TG))
    grad_in(0)

    for level in range(5, 8):
        gather(level)
    for level in range(4, 8):
        finish(level, fin, level - 4)
    for level in range(4, 8):
        arrived(fin.at[level - 4], S_FS + level)

    def pack(h):
        for lv in range(4):
            hs[h, lv] = fin[lv, h].reshape(16, 128).astype(BF)

    loop(16, pack)
    to_tensor(lambda j: hs.at[j], hr.at[t], S_HA)

    for level in (3, 2, 1, 0):
        gather(level)
    for level in (3, 2, 1, 0):
        finish(level, fgrad, level)

    arrived(hr, S_HA)

    def unpack(j):
        for lv in range(4):
            ob[lv, j] = hr[j, lv].astype(F32).reshape(2, 8, 128)

    loop(16, unpack)
    local(ob, fgrad.at[pl.ds(4, 4)], S_OB)

    for level in range(4):
        arrived(fgrad.at[level], S_FS + level)
    arrived(mixed, S_MA)
    arrived(tgrad, S_TG)
    arrived(fgrad.at[pl.ds(4, 4)], S_OB)
    blocks = xo.at[0, pl.ds(0, 15)]
    for slot in (S_CA, S_XA, S_GA, S_MA):
        left(blocks, slot)
    left(hs.at[pl.ds(0, 15)], S_FZ)
    left(hs.at[pl.ds(0, 15)], S_HA)
    for lv in range(4):
        left(wt.at[lv, 0, 0, 0], S_AX + lv)
        left(wt.at[lv, 0, :, pl.ds(0, 3)], S_AY + lv)
        left(wt.at[lv, 0], S_CF + lv)
    for level in range(8):
        left(csend.at[level], S_CD + level)
        left(part.at[level, :, pl.ds(0, 3)], S_RY + level)
        left(mid.at[level], S_RX + level)
        left(acc.at[level, :, :, pl.ds(0, 8)], S_FS + level)


def per_device(tokens, factors, cotangent):
    hbm = pl.BlockSpec(memory_space=pl.ANY)
    acts = pltpu.VMEM((5, 16, 128, 128), BF)
    grads = pltpu.VMEM((8, 2, 4, 8, 2, 16, 128), BF)
    slab = pltpu.VMEM((8, 8, 2, 16, 128), BF)
    return pl.pallas_call(
        kernel,
        out_shape=(
            jax.ShapeDtypeStruct((128, 2048), BF),
            jax.ShapeDtypeStruct((128, 2048), BF),
            jax.ShapeDtypeStruct((8, 16, 2, 8, 128), F32),
        ),
        in_specs=[hbm] * 3,
        out_specs=[hbm] * 3,
        scratch_shapes=[
            acts, acts, acts, acts,
            pltpu.VMEM((4, 16, 2, 128, 128), BF),
            pltpu.VMEM((4, 2, 2, 4, 16, 16, 128), BF),
            grads, grads, grads, grads, slab, slab,
            pltpu.VMEM((8, 8, 2, 16, 128), F32),
            pltpu.VMEM((4, 16, 2, 8, 128), F32),
            pltpu.VMEM((16, 4, 16, 128), BF),
            pltpu.VMEM((16, 4, 16, 128), BF),
            pltpu.VMEM((4, 16, 2, 8, 128), F32),
            pltpu.SemaphoreType.DMA((N_SEM,)),
            pltpu.SemaphoreType.DMA((N_SEM,)),
        ],
        compiler_params=pltpu.CompilerParams(
            collective_id=0, has_side_effects=True, vmem_limit_bytes=56 * 1024 * 1024
        ),
        cost_estimate=pl.CostEstimate(flops=3221225472, bytes_accessed=12582912, transcendentals=0),
        name="butterfly",
    )(tokens, factors, cotangent)


def solution(mesh):
    placed = (P("dp", "tensor"), P(None, "tensor", None, None, None), P("dp", "tensor"))
    return jax.shard_map(
        per_device,
        mesh=mesh,
        in_specs=placed,
        out_specs=(P("dp", "tensor"), P("dp", "tensor"), P(None, "tensor", None, "dp", None)),
        check_vma=False,
    )
```

```python
import jax
import jax.numpy as jnp
from jax import lax
from jax.experimental import pallas as pl
from jax.experimental.pallas import tpu as pltpu
from jax.sharding import PartitionSpec as P

MESH = pl.DeviceIdType.MESH
BF = jnp.bfloat16
F32 = jnp.float32

S_X0, S_W, S_FZ, S_CA, S_XA, S_GA, S_MA, S_HA, S_TG, S_OB = range(10)
S_AX, S_AY, S_AR, S_CF, S_CD, S_RR, S_RY, S_RX, S_FS = 10, 14, 18, 22, 26, 34, 42, 50, 58
S_FY, N_SEM = 66, 67


def pair(q, d):
    return (q // d) * (2 * d) + q % d


def wide(a, b):
    return jnp.concatenate([a, b], axis=1)


def kernel(
    tok, fac, cot, mixed, tgrad, fgrad,
    xo, xt, go, gt, w, wt, csend, crecv, part, rel, rsum, got, mid, other, acc, fin, hs, hr, ob,
    rsem, ssem,
):
    dp, t = lax.axis_index("dp"), lax.axis_index("tensor")
    c, s = dp % 2, dp // 2
    oc = 1 - c
    xl, y = s // 4, s % 4

    def far(k):
        return (t + 8 + ((k + 1) // 2) * (1 - 2 * (k % 2))) % 16

    def along(i):
        return (y + i) % 4

    def send(src, dst, slot, device):
        pltpu.make_async_remote_copy(
            src_ref=src, dst_ref=dst, send_sem=ssem.at[slot], recv_sem=rsem.at[slot],
            device_id=device, device_id_type=MESH,
        ).start()

    def local(src, dst, slot):
        pltpu.make_async_copy(src, dst, rsem.at[slot]).start()

    def arrived(ref, slot):
        pltpu.make_async_copy(ref, ref, rsem.at[slot]).wait()

    def left(ref, slot):
        pltpu.make_async_copy(ref, ref, ssem.at[slot]).wait()

    def loop(n, body, unroll=1):
        def step(i, carry):
            body(i)
            return carry

        lax.fori_loop(0, n, step, 0, unroll=unroll)

    sibling = (s * 2 + oc, t)
    across = ((s + 4) % 8 * 2 + c, t)

    def to_tensor(src, dst, slot):
        loop(15, lambda k: send(src(far(k)), dst, slot, (dp, far(k))))
        local(src(t), dst, slot)

    up, down = along(1), along(3)
    above = ((xl * 4 + up) * 2 + c, t)
    below = ((xl * 4 + down) * 2 + c, t)

    barrier = pltpu.get_barrier_semaphore()

    def greet(device):
        pl.semaphore_signal(barrier, inc=1, device_id=device, device_id_type=MESH)

    loop(15, lambda k: greet((dp, far(k))))
    greet(above)
    greet(below)
    greet(across)
    greet(sibling)
    loop(16, lambda j: local(tok.at[:, pl.ds(pl.multiple_of(j * 128, 128), 128)], xo.at[0, j], S_X0))
    local(fac.at[pl.ds(0, 4)], w, S_W)

    pl.semaphore_wait(barrier, 19)

    rows = pl.ds(pl.multiple_of(s * 16, 16), 16)
    to_tensor(lambda j: fac.at[7, j, c, rows, :], wt.at[3, c, xl, y, t], S_FZ)
    to_tensor(lambda j: fac.at[pl.ds(4, 3), j, c, rows, :], wt.at[pl.ds(0, 3), c, xl, y, t], S_FY)
    to_tensor(
        lambda j: cot.at[:, pl.ds(pl.multiple_of(j * 128, 128), 128)], gt.at[4, t], S_CA
    )

    def weights_low(level):
        return lambda b, k: w[level, b, k]

    def weights_high(lv):
        return lambda b, k: wt[lv, k, :, :, b].reshape(128, 128)

    def matrix(weights, b0, b1):
        return jnp.concatenate(
            [wide(weights(b0, 0), weights(b1, 1)), wide(weights(b0, 1), weights(b1, 0))], axis=0
        )

    def forward(x, at, d, weights):
        def body(q):
            b0 = pair(q, d)
            b1 = b0 + d
            new = jnp.dot(
                wide(x[at, b0], x[at, b1]), matrix(weights, b0, b1), preferred_element_type=F32
            ).astype(BF)
            x[at + 1, b0] = new[:, :128]
            x[at + 1, b1] = new[:, 128:]

        loop(8, body, 8)

    def backward(g, at, d, weights):
        def body(q):
            b0 = pair(q, d)
            b1 = b0 + d
            new = lax.dot_general(
                wide(g[at + 1, b0], g[at + 1, b1]), matrix(weights, b0, b1),
                (((1,), (1,)), ((), ())), preferred_element_type=F32,
            ).astype(BF)
            g[at, b0] = new[:, :128]
            g[at, b1] = new[:, 128:]

        loop(8, body, 8)

    def gradient(x, g, at, d, core, put):
        dl = min(d, 4)

        def body(q):
            b0 = pair(core * 4 + q, d)
            b1 = b0 + d
            dm = lax.dot_general(
                wide(x[at, b0], x[at, b1]), wide(g[at + 1, b0], g[at + 1, b1]),
                (((0,), (0,)), ((), ())), preferred_element_type=F32,
            )
            m0 = pair(q, dl)
            m1 = m0 + dl
            put(m0, 0, dm[:128, :128].reshape(2, 4, 16, 128))
            put(m0, 1, dm[128:, :128].reshape(2, 4, 16, 128))
            put(m1, 1, dm[:128, 128:].reshape(2, 4, 16, 128))
            put(m1, 0, dm[128:, 128:].reshape(2, 4, 16, 128))

        loop(4, body, 4)

    def side(level):
        return (xo, go, level) if level < 4 else (xt, gt, level - 4)

    def grad_out(level):
        x, g, at = side(level)

        def put(m, k, value):
            csend[level, :, :, m, k] = value.astype(BF)

        gradient(x, g, at, 2**at, oc, put)
        send(csend.at[level], crecv.at[level], S_CD + level, sibling)

    def grad_in(level):
        x, g, at = side(level)
        arrived(crecv.at[level], S_CD + level)

        def put(m, k, value):
            part[level, :, :, m, k] = (value + crecv[level, :, :, m, k].astype(F32)).astype(BF)

        gradient(x, g, at, 2**at, c, put)
        send(part.at[level, 0, along(2)], rel.at[level, 0], S_RR + level, above)
        send(part.at[level, 1, along(2)], rel.at[level, 1], S_RR + level, below)
        send(part.at[level, 1, up], got.at[level, 1, 0], S_RY + level, above)
        send(part.at[level, 0, down], got.at[level, 0, 0], S_RY + level, below)

    def relay(level):
        arrived(rel.at[level], S_RR + level)

        def body(m):
            for u, way in ((0, up), (1, down)):
                value = rel[level, u, m].astype(F32) + part[level, u, way, m].astype(F32)
                rsum[level, u, m] = value.astype(BF)

        loop(8, body, 4)
        send(rsum.at[level, 0], got.at[level, 0, 1], S_RY + level, above)
        send(rsum.at[level, 1], got.at[level, 1, 1], S_RY + level, below)

    def gather(level):
        arrived(got.at[level], S_RY + level)

        def total(side_of, m):
            value = part[level, side_of, y, m].astype(F32)
            for i in range(2):
                value = value + got[level, side_of, i, m].astype(F32)
            return value

        def give(m):
            mid[level, m] = total(1 - xl, m).astype(BF)

        def keep(m):
            acc[level, m] = total(xl, m)

        loop(8, give, 4)
        send(mid.at[level], other.at[level], S_RX + level, across)
        loop(8, keep, 4)

    def finish(level, out, at):
        arrived(other.at[level], S_RX + level)

        def body(m):
            acc[level, m] = acc[level, m] + other[level, m].astype(F32)

        loop(8, body, 4)
        for u in range(2):
            first = 8 * c + 4 * u if level % 4 < 3 else 8 * u + 4 * c
            dst = out.at[at, pl.ds(first, 4)]
            mine = pl.ds(pl.multiple_of(c * 8, 8), 8)
            theirs = pl.ds(pl.multiple_of(oc * 8, 8), 8)
            local(acc.at[level, pl.ds(4 * u, 4), :, mine], dst, S_FS + level)
            send(acc.at[level, pl.ds(4 * u, 4), :, theirs], dst, S_FS + level, sibling)

    arrived(xo.at[0], S_X0)
    arrived(w, S_W)
    for level in range(4):
        forward(xo, level, 2**level, weights_low(level))

    to_tensor(lambda j: xo.at[4, j], xt.at[0, t], S_XA)

    def share(lv):
        piece = wt.at[lv, c, xl, y]
        send(piece, piece, S_AX + lv, across)
        send(piece, piece, S_AY + lv, above)
        send(piece, piece, S_AY + lv, below)

    def share_more(lv):
        piece = wt.at[lv, c, 1 - xl, y]
        arrived(piece, S_AX + lv)
        send(piece, piece, S_AY + lv, above)
        send(piece, piece, S_AY + lv, below)

    def share_on(lv):
        arrived(wt.at[lv, c, :, pl.ds(0, 2)], S_AY + lv)
        first, second = wt.at[lv, c, 0, down], wt.at[lv, c, 1, up]
        send(first, first, S_AR + lv, above)
        send(second, second, S_AR + lv, below)

    def pass_on(lv):
        arrived(wt.at[lv, c, :, 0], S_AR + lv)
        send(wt.at[lv, c], wt.at[lv, c], S_CF + lv, sibling)

    arrived(wt.at[0, c, xl, y], S_FZ)
    share(3)
    arrived(wt.at[pl.ds(0, 3), c, xl, y], S_FY)
    share(2)
    share_more(3)
    share(1)
    share(0)
    share_more(2)
    share_on(3)
    share_more(1)
    share_more(0)
    share_on(2)
    pass_on(3)
    arrived(gt.at[4], S_CA)
    for lv in (3, 2, 1, 0):
        if lv > 1:
            share_on(lv - 2)
        if lv > 0:
            pass_on(lv - 1)
        arrived(wt.at[lv, oc], S_CF + lv)
        backward(gt, lv, 2**lv, weights_high(lv))
    to_tensor(lambda j: gt.at[0, j], go.at[4, t], S_GA)

    arrived(xt.at[0], S_XA)
    for level in range(4, 8):
        grad_out(level)
        forward(xt, level - 4, 2 ** (level - 4), weights_high(level - 4))
        if level > 4:
            grad_in(level - 1)
        if level > 5:
            relay(level - 2)
    to_tensor(lambda j: xt.at[4, j], mixed.at[:, pl.ds(pl.multiple_of(t * 128, 128), 128)], S_MA)
    grad_in(7)

    relay(6)
    gather(4)

    arrived(go.at[4], S_GA)
    for level in (3, 2, 1, 0):
        grad_out(level)
        backward(go, level, 2**level, weights_low(level))
        grad_in(level)
        relay(7 if level == 3 else level + 1)
        if level > 0:
            gather(8 - level)
    loop(16, lambda j: local(go.at[0, j], tgrad.at[:, pl.ds(pl.multiple_of(j * 128, 128), 128)], S_TG))

    for level in range(4, 8):
        finish(level, fin, level - 4)
    for level in range(4, 8):
        arrived(fin.at[level - 4], S_FS + level)

    def pack(h):
        for lv in range(4):
            hs[h, lv] = fin[lv, h].reshape(16, 128).astype(BF)

    loop(16, pack)
    to_tensor(lambda j: hs.at[j], hr.at[t], S_HA)

    gather(3)
    relay(0)
    gather(2)
    finish(3, fgrad, 3)
    gather(1)
    finish(2, fgrad, 2)
    gather(0)
    finish(1, fgrad, 1)
    finish(0, fgrad, 0)

    arrived(hr, S_HA)

    def unpack(j):
        for lv in range(4):
            ob[lv, j] = hr[j, lv].astype(F32).reshape(2, 8, 128)

    loop(16, unpack)
    local(ob, fgrad.at[pl.ds(4, 4)], S_OB)

    for level in range(4):
        arrived(fgrad.at[level], S_FS + level)
    arrived(mixed, S_MA)
    arrived(tgrad, S_TG)
    arrived(fgrad.at[pl.ds(4, 4)], S_OB)
    blocks = xo.at[0, pl.ds(0, 15)]
    for slot in (S_CA, S_XA, S_GA, S_MA):
        left(blocks, slot)
    left(hs.at[pl.ds(0, 15), 0], S_FZ)
    left(hs.at[pl.ds(0, 15), pl.ds(0, 3)], S_FY)
    left(hs.at[pl.ds(0, 15)], S_HA)
    for lv in range(4):
        left(wt.at[lv, 0, 0, 0], S_AX + lv)
        left(wt.at[lv, 0, :, pl.ds(0, 2)], S_AY + lv)
        left(wt.at[lv, 0, :, 0], S_AR + lv)
        left(wt.at[lv, 0], S_CF + lv)
    for level in range(8):
        left(csend.at[level], S_CD + level)
        left(rel.at[level], S_RR + level)
        left(got.at[level], S_RY + level)
        left(mid.at[level], S_RX + level)
        left(acc.at[level, :, :, pl.ds(0, 8)], S_FS + level)


def hand_over(a, b, c, a_out, b_out, c_out, a_held, b_held, c_held, sem):
    moves = ((c, c_held, c_out), (a, a_held, a_out), (b, b_held, b_out))
    into = [pltpu.make_async_copy(m[0], m[1], sem.at[i]) for i, m in enumerate(moves)]
    out = [pltpu.make_async_copy(m[1], m[2], sem.at[3 + i]) for i, m in enumerate(moves)]
    for copy in into:
        copy.start()
    for i in range(3):
        into[i].wait()
        out[i].start()
    for copy in out:
        copy.wait()


def per_device(tokens, factors, cotangent):
    hbm = pl.BlockSpec(memory_space=pl.ANY)
    acts = pltpu.VMEM((5, 16, 128, 128), BF)
    grads = pltpu.VMEM((8, 2, 4, 8, 2, 16, 128), BF)
    slab = pltpu.VMEM((8, 8, 2, 16, 128), BF)
    two = pltpu.VMEM((8, 2, 8, 2, 16, 128), BF)
    shapes = (
        jax.ShapeDtypeStruct((128, 2048), BF),
        jax.ShapeDtypeStruct((128, 2048), BF),
        jax.ShapeDtypeStruct((8, 16, 2, 8, 128), F32),
    )
    results = pl.pallas_call(
        kernel,
        out_shape=shapes,
        in_specs=[hbm] * 3,
        out_specs=[hbm] * 3,
        scratch_shapes=[
            acts, acts, acts, acts,
            pltpu.VMEM((4, 16, 2, 128, 128), BF),
            pltpu.VMEM((4, 2, 2, 4, 16, 16, 128), BF),
            grads, grads, grads, two, two, pltpu.VMEM((8, 2, 2, 8, 2, 16, 128), BF), slab, slab,
            pltpu.VMEM((8, 8, 2, 16, 128), F32),
            pltpu.VMEM((4, 16, 2, 8, 128), F32),
            pltpu.VMEM((16, 4, 16, 128), BF),
            pltpu.VMEM((16, 4, 16, 128), BF),
            pltpu.VMEM((4, 16, 2, 8, 128), F32),
            pltpu.SemaphoreType.DMA((N_SEM,)),
            pltpu.SemaphoreType.DMA((N_SEM,)),
        ],
        compiler_params=pltpu.CompilerParams(
            collective_id=0, has_side_effects=True, vmem_limit_bytes=56 * 1024 * 1024
        ),
        cost_estimate=pl.CostEstimate(flops=3221225472, bytes_accessed=12582912, transcendentals=0),
        name="butterfly",
    )(tokens, factors, cotangent)
    return pl.pallas_call(
        hand_over,
        out_shape=shapes,
        in_specs=[hbm] * 3,
        out_specs=[hbm] * 3,
        scratch_shapes=[pltpu.VMEM(x.shape, x.dtype) for x in shapes] + [pltpu.SemaphoreType.DMA((6,))],
        name="hand_over",
    )(*results)


def solution(mesh):
    placed = (P("dp", "tensor"), P(None, "tensor", None, None, None), P("dp", "tensor"))
    return jax.shard_map(
        per_device,
        mesh=mesh,
        in_specs=placed,
        out_specs=(P("dp", "tensor"), P("dp", "tensor"), P(None, "tensor", None, "dp", None)),
        check_vma=False,
    )
```

```python
import jax
import jax.numpy as jnp
from jax import lax
from jax.experimental import pallas as pl
from jax.experimental.pallas import tpu as pltpu
from jax.sharding import PartitionSpec as P

MESH = pl.DeviceIdType.MESH
BF = jnp.bfloat16
F32 = jnp.float32

S_X0, S_W, S_FZ, S_CA, S_XA, S_GA, S_MA, S_HA, S_TG, S_OB = range(10)
S_AX, S_AY, S_AR, S_CF, S_CD, S_RR, S_RY, S_RX, S_FS = 10, 14, 18, 22, 26, 34, 42, 50, 58
S_FY, S_HB, S_OC, N_SEM = 66, 67, 68, 69
ACROSS_FIRST = ()
ORDER = (
    "o4", "f4", "o5", "f5", "i4", "o6", "f6", "i5", "r4", "o7", "f7", "i6", "r5", "M0",
    "i7", "r6", "g4", "G0", "o3", "b3", "i3", "r7", "g5", "o2", "b2", "i2", "r3", "g6",
    "e4", "e5", "o1", "b1", "i1", "r2", "g7", "H0", "o0", "b0", "i0", "e6", "e7", "r1",
    "T0", "H1", "g3", "r0", "g2", "e3", "g1", "e2", "I0", "g0", "e1", "I1", "e0",
)


def pair(q, d):
    return (q // d) * (2 * d) + q % d


def wide(a, b):
    return jnp.concatenate([a, b], axis=1)


def kernel(
    tok, fac, cot, mixed, tgrad, fgrad,
    xo, xt, go, gt, w, wt, csend, crecv, part, rel, rsum, got, mid, other, xin, acc, fin, hs, hr, ob,
    rsem, ssem,
):
    dp, t = lax.axis_index("dp"), lax.axis_index("tensor")
    c, s = dp % 2, dp // 2
    oc = 1 - c
    xl, y = s // 4, s % 4

    def far(k):
        return (t + 8 + ((k + 1) // 2) * (1 - 2 * (k % 2))) % 16

    def along(i):
        return (y + i) % 4

    def send(src, dst, slot, device):
        pltpu.make_async_remote_copy(
            src_ref=src, dst_ref=dst, send_sem=ssem.at[slot], recv_sem=rsem.at[slot],
            device_id=device, device_id_type=MESH,
        ).start()

    def local(src, dst, slot):
        pltpu.make_async_copy(src, dst, rsem.at[slot]).start()

    def arrived(ref, slot):
        pltpu.make_async_copy(ref, ref, rsem.at[slot]).wait()

    def left(ref, slot):
        pltpu.make_async_copy(ref, ref, ssem.at[slot]).wait()

    def loop(n, body, unroll=1):
        def step(i, carry):
            body(i)
            return carry

        lax.fori_loop(0, n, step, 0, unroll=unroll)

    sibling = (s * 2 + oc, t)
    across = ((s + 4) % 8 * 2 + c, t)

    def to_tensor(src, dst, slot):
        loop(15, lambda k: send(src(far(k)), dst, slot, (dp, far(k))))
        local(src(t), dst, slot)

    def span(level):
        return 4 if level in ACROSS_FIRST else 8

    up, down = along(1), along(3)
    above = ((xl * 4 + up) * 2 + c, t)
    below = ((xl * 4 + down) * 2 + c, t)

    barrier = pltpu.get_barrier_semaphore()

    def greet(device):
        pl.semaphore_signal(barrier, inc=1, device_id=device, device_id_type=MESH)

    loop(15, lambda k: greet((dp, far(k))))
    greet(above)
    greet(below)
    greet(across)
    greet(sibling)
    loop(16, lambda j: local(tok.at[:, pl.ds(pl.multiple_of(j * 128, 128), 128)], xo.at[0, j], S_X0))
    local(fac.at[pl.ds(0, 4)], w, S_W)

    pl.semaphore_wait(barrier, 19)

    rows = pl.ds(pl.multiple_of(s * 16, 16), 16)

    to_tensor(lambda j: fac.at[7, j, c, rows, :], wt.at[3, c, xl, y, t], S_FZ)
    to_tensor(lambda j: fac.at[pl.ds(4, 3), j, c, rows, :], wt.at[pl.ds(0, 3), c, xl, y, t], S_FY)
    to_tensor(
        lambda j: cot.at[:, pl.ds(pl.multiple_of(j * 128, 128), 128)], gt.at[4, t], S_CA
    )

    def weights_low(level):
        return lambda b, k: w[level, b, k]

    def weights_high(lv):
        return lambda b, k: wt[lv, k, :, :, b].reshape(128, 128)

    def matrix(weights, b0, b1):
        return jnp.concatenate(
            [wide(weights(b0, 0), weights(b1, 1)), wide(weights(b0, 1), weights(b1, 0))], axis=0
        )

    def forward(x, at, d, weights):
        def body(q):
            b0 = pair(q, d)
            b1 = b0 + d
            new = jnp.dot(
                wide(x[at, b0], x[at, b1]), matrix(weights, b0, b1), preferred_element_type=F32
            ).astype(BF)
            x[at + 1, b0] = new[:, :128]
            x[at + 1, b1] = new[:, 128:]

        loop(8, body, 8)

    def backward(g, at, d, weights):
        def body(q):
            b0 = pair(q, d)
            b1 = b0 + d
            new = lax.dot_general(
                wide(g[at + 1, b0], g[at + 1, b1]), matrix(weights, b0, b1),
                (((1,), (1,)), ((), ())), preferred_element_type=F32,
            ).astype(BF)
            g[at, b0] = new[:, :128]
            g[at, b1] = new[:, 128:]

        loop(8, body, 8)

    def gradient(x, g, at, d, core, put):
        dl = min(d, 4)

        def body(q):
            b0 = pair(core * 4 + q, d)
            b1 = b0 + d
            dm = lax.dot_general(
                wide(x[at, b0], x[at, b1]), wide(g[at + 1, b0], g[at + 1, b1]),
                (((0,), (0,)), ((), ())), preferred_element_type=F32,
            )
            m0 = pair(q, dl)
            m1 = m0 + dl
            put(m0, 0, dm[:128, :128].reshape(2, 4, 16, 128))
            put(m0, 1, dm[128:, :128].reshape(2, 4, 16, 128))
            put(m1, 1, dm[:128, 128:].reshape(2, 4, 16, 128))
            put(m1, 0, dm[128:, 128:].reshape(2, 4, 16, 128))

        loop(4, body, 4)

    def side(level):
        return (xo, go, level) if level < 4 else (xt, gt, level - 4)

    def grad_out(level):
        x, g, at = side(level)

        def put(m, k, value):
            csend[level, :, :, m, k] = value.astype(BF)

        gradient(x, g, at, 2**at, oc, put)
        send(csend.at[level], crecv.at[level], S_CD + level, sibling)

    def grad_in(level):
        x, g, at = side(level)
        arrived(crecv.at[level], S_CD + level)

        def put(m, k, value):
            part[level, :, :, m, k] = (value + crecv[level, :, :, m, k].astype(F32)).astype(BF)

        gradient(x, g, at, 2**at, c, put)
        if level in ACROSS_FIRST:
            send(part.at[level, 1 - xl], xin.at[level], S_RX + level, across)
        else:
            set_off(level)

    def ways(level):
        return ((xl, 0), (xl, 4)) if level in ACROSS_FIRST else ((0, 0), (1, 0))

    def set_off(level):
        n = span(level)
        (us, um), (ds, dm) = ways(level)
        head = pl.ds(0, n)

        def piece(side_of, way, first):
            return part.at[level, side_of, way, pl.ds(first, n)]

        send(piece(us, along(2), um), rel.at[level, 0, head], S_RR + level, above)
        send(piece(ds, along(2), dm), rel.at[level, 1, head], S_RR + level, below)
        send(piece(ds, up, dm), got.at[level, 1, 0, head], S_RY + level, above)
        send(piece(us, down, um), got.at[level, 0, 0, head], S_RY + level, below)

    def meet(level):
        if level not in ACROSS_FIRST:
            return
        arrived(xin.at[level], S_RX + level)

        def body(m):
            for i in range(4):
                value = part[level, xl, i, m].astype(F32) + xin[level, i, m].astype(F32)
                part[level, xl, i, m] = value.astype(BF)

        loop(8, body, 4)
        set_off(level)

    def relay(level):
        n = span(level)
        (us, um), (ds, dm) = ways(level)
        head = pl.ds(0, n)
        arrived(rel.at[level, :, head], S_RR + level)

        def body(m):
            first = rel[level, 0, m].astype(F32) + part[level, us, up, um + m].astype(F32)
            second = rel[level, 1, m].astype(F32) + part[level, ds, down, dm + m].astype(F32)
            rsum[level, 0, m] = first.astype(BF)
            rsum[level, 1, m] = second.astype(BF)

        loop(n, body, 4)
        send(rsum.at[level, 0, head], got.at[level, 0, 1, head], S_RY + level, above)
        send(rsum.at[level, 1, head], got.at[level, 1, 1, head], S_RY + level, below)

    def gather(level):
        n = span(level)
        arrived(got.at[level, :, :, pl.ds(0, n)], S_RY + level)

        def total(side_of, half, first, m):
            value = part[level, side_of, y, first + m].astype(F32)
            for i in range(2):
                value = value + got[level, half, i, m].astype(F32)
            return value

        if level in ACROSS_FIRST:

            def both(m):
                acc[level, m] = total(xl, 0, 0, m)
                acc[level, 4 + m] = total(xl, 1, 4, m)

            loop(4, both, 4)
            return

        def give(m):
            mid[level, m] = total(1 - xl, 1 - xl, 0, m).astype(BF)

        def keep(m):
            acc[level, m] = total(xl, xl, 0, m)

        loop(8, give, 4)
        send(mid.at[level], other.at[level], S_RX + level, across)
        loop(8, keep, 4)

    def finish(level, out, at):
        if level not in ACROSS_FIRST:
            arrived(other.at[level], S_RX + level)

            def body(m):
                acc[level, m] = acc[level, m] + other[level, m].astype(F32)

            loop(8, body, 4)
        for u in range(2):
            first = 8 * c + 4 * u if level % 4 < 3 else 8 * u + 4 * c
            dst = out.at[at, pl.ds(first, 4)]
            mine = pl.ds(pl.multiple_of(c * 8, 8), 8)
            theirs = pl.ds(pl.multiple_of(oc * 8, 8), 8)
            local(acc.at[level, pl.ds(4 * u, 4), :, mine], dst, S_FS + level)
            send(acc.at[level, pl.ds(4 * u, 4), :, theirs], dst, S_FS + level, sibling)

    arrived(xo.at[0], S_X0)
    arrived(w, S_W)
    for level in range(4):
        forward(xo, level, 2**level, weights_low(level))

    to_tensor(lambda j: xo.at[4, j], xt.at[0, t], S_XA)

    def share(lv):
        piece = wt.at[lv, c, xl, y]
        send(piece, piece, S_AX + lv, across)
        send(piece, piece, S_AY + lv, above)
        send(piece, piece, S_AY + lv, below)

    def share_more(lv):
        piece = wt.at[lv, c, 1 - xl, y]
        arrived(piece, S_AX + lv)
        send(piece, piece, S_AY + lv, above)
        send(piece, piece, S_AY + lv, below)

    def share_on(lv):
        arrived(wt.at[lv, c, :, pl.ds(0, 2)], S_AY + lv)
        first, second = wt.at[lv, c, 0, down], wt.at[lv, c, 1, up]
        send(first, first, S_AR + lv, above)
        send(second, second, S_AR + lv, below)

    def pass_on(lv):
        arrived(wt.at[lv, c, :, 0], S_AR + lv)
        send(wt.at[lv, c], wt.at[lv, c], S_CF + lv, sibling)

    arrived(wt.at[0, c, xl, y], S_FZ)
    share(3)
    arrived(wt.at[pl.ds(0, 3), c, xl, y], S_FY)
    share(2)
    share_more(3)
    share(1)
    share(0)
    share_more(2)
    share_on(3)
    share_more(1)
    share_more(0)
    share_on(2)
    pass_on(3)
    arrived(gt.at[4], S_CA)
    for lv in (3, 2, 1, 0):
        if lv > 1:
            share_on(lv - 2)
        if lv > 0:
            pass_on(lv - 1)
        arrived(wt.at[lv, oc], S_CF + lv)
        backward(gt, lv, 2**lv, weights_high(lv))
    to_tensor(lambda j: gt.at[0, j], go.at[4, t], S_GA)

    def forth(level):
        forward(xt, level - 4, 2 ** (level - 4), weights_high(level - 4))

    def back(level):
        backward(go, level, 2**level, weights_low(level))

    def end(level):
        finish(level, *((fgrad, level) if level < 4 else (fin, level - 4)))

    def mix_out(_):
        own = pl.ds(pl.multiple_of(t * 128, 128), 128)
        to_tensor(lambda j: xt.at[4, j], mixed.at[:, own], S_MA)

    def grad_home(_):
        arrived(go.at[4], S_GA)

    def token_out(_):
        loop(16, lambda j: local(go.at[0, j], tgrad.at[:, pl.ds(pl.multiple_of(j * 128, 128), 128)], S_TG))

    def high_out(g):
        for lv in (2 * g, 2 * g + 1):
            arrived(fin.at[lv], S_FS + 4 + lv)

        def pack(h):
            for lv in (2 * g, 2 * g + 1):
                hs[h, lv] = fin[lv, h].reshape(16, 128).astype(BF)

        loop(16, pack, 4)
        two = pl.ds(2 * g, 2)
        to_tensor(lambda j: hs.at[j, two], hr.at[t, two], (S_HA, S_HB)[g])

    def high_in(g):
        two = pl.ds(2 * g, 2)
        arrived(hr.at[:, two], (S_HA, S_HB)[g])

        def unpack(j):
            for lv in (2 * g, 2 * g + 1):
                ob[lv, j] = hr[j, lv].astype(F32).reshape(2, 8, 128)

        loop(16, unpack, 4)
        local(ob.at[two], fgrad.at[pl.ds(4 + 2 * g, 2)], (S_OB, S_OC)[g])

    steps = dict(
        o=grad_out, i=grad_in, f=forth, b=back, r=relay, g=gather, m=meet, e=end,
        M=mix_out, G=grad_home, T=token_out, H=high_out, I=high_in,
    )
    arrived(xt.at[0], S_XA)
    for step in ORDER:
        steps[step[0]](int(step[1]))

    for level in range(4):
        arrived(fgrad.at[level], S_FS + level)
    arrived(mixed, S_MA)
    arrived(tgrad, S_TG)
    arrived(fgrad.at[pl.ds(4, 2)], S_OB)
    arrived(fgrad.at[pl.ds(6, 2)], S_OC)
    blocks = xo.at[0, pl.ds(0, 15)]
    for slot in (S_CA, S_XA, S_GA, S_MA):
        left(blocks, slot)
    left(hs.at[pl.ds(0, 15), 0], S_FZ)
    left(hs.at[pl.ds(0, 15), pl.ds(0, 3)], S_FY)
    left(hs.at[pl.ds(0, 15), pl.ds(0, 2)], S_HA)
    left(hs.at[pl.ds(0, 15), pl.ds(0, 2)], S_HB)
    for lv in range(4):
        left(wt.at[lv, 0, 0, 0], S_AX + lv)
        left(wt.at[lv, 0, :, pl.ds(0, 2)], S_AY + lv)
        left(wt.at[lv, 0, :, 0], S_AR + lv)
        left(wt.at[lv, 0], S_CF + lv)
    for level in range(8):
        left(csend.at[level], S_CD + level)
        left(rel.at[level, :, pl.ds(0, span(level))], S_RR + level)
        left(got.at[level, :, :, pl.ds(0, span(level))], S_RY + level)
        left(part.at[level, 0] if level in ACROSS_FIRST else mid.at[level], S_RX + level)
        left(acc.at[level, :, :, pl.ds(0, 8)], S_FS + level)


def hand_over(a, b, c, a_out, b_out, c_out, a_held, b_held, c_held, sem):
    moves = ((c, c_held, c_out), (a, a_held, a_out), (b, b_held, b_out))
    into = [pltpu.make_async_copy(m[0], m[1], sem.at[i]) for i, m in enumerate(moves)]
    out = [pltpu.make_async_copy(m[1], m[2], sem.at[3 + i]) for i, m in enumerate(moves)]
    for copy in into:
        copy.start()
    for i in range(3):
        into[i].wait()
        out[i].start()
    for copy in out:
        copy.wait()


def per_device(tokens, factors, cotangent):
    hbm = pl.BlockSpec(memory_space=pl.ANY)
    acts = pltpu.VMEM((5, 16, 128, 128), BF)
    grads = pltpu.VMEM((8, 2, 4, 8, 2, 16, 128), BF)
    slab = pltpu.VMEM((8, 8, 2, 16, 128), BF)
    two = pltpu.VMEM((8, 2, 8, 2, 16, 128), BF)
    shapes = (
        jax.ShapeDtypeStruct((128, 2048), BF),
        jax.ShapeDtypeStruct((128, 2048), BF),
        jax.ShapeDtypeStruct((8, 16, 2, 8, 128), F32),
    )
    results = pl.pallas_call(
        kernel,
        out_shape=shapes,
        in_specs=[hbm] * 3,
        out_specs=[hbm] * 3,
        scratch_shapes=[
            acts, acts, acts, acts,
            pltpu.VMEM((4, 16, 2, 128, 128), BF),
            pltpu.VMEM((4, 2, 2, 4, 16, 16, 128), BF),
            grads, grads, grads, two, two, pltpu.VMEM((8, 2, 2, 8, 2, 16, 128), BF), slab, slab,
            pltpu.VMEM((2, 4, 8, 2, 16, 128), BF),
            pltpu.VMEM((8, 8, 2, 16, 128), F32),
            pltpu.VMEM((4, 16, 2, 8, 128), F32),
            pltpu.VMEM((16, 4, 16, 128), BF),
            pltpu.VMEM((16, 4, 16, 128), BF),
            pltpu.VMEM((4, 16, 2, 8, 128), F32),
            pltpu.SemaphoreType.DMA((N_SEM,)),
            pltpu.SemaphoreType.DMA((N_SEM,)),
        ],
        compiler_params=pltpu.CompilerParams(
            collective_id=0, has_side_effects=True, vmem_limit_bytes=56 * 1024 * 1024
        ),
        cost_estimate=pl.CostEstimate(flops=3221225472, bytes_accessed=12582912, transcendentals=0),
        name="butterfly",
    )(tokens, factors, cotangent)
    return pl.pallas_call(
        hand_over,
        out_shape=shapes,
        in_specs=[hbm] * 3,
        out_specs=[hbm] * 3,
        scratch_shapes=[pltpu.VMEM(x.shape, x.dtype) for x in shapes] + [pltpu.SemaphoreType.DMA((6,))],
        name="hand_over",
    )(*results)


def solution(mesh):
    placed = (P("dp", "tensor"), P(None, "tensor", None, None, None), P("dp", "tensor"))
    return jax.shard_map(
        per_device,
        mesh=mesh,
        in_specs=placed,
        out_specs=(P("dp", "tensor"), P("dp", "tensor"), P(None, "tensor", None, "dp", None)),
        check_vma=False,
    )
```

```python
import jax
import jax.numpy as jnp
from jax import lax
from jax.experimental import pallas as pl
from jax.experimental.pallas import tpu as pltpu
from jax.sharding import PartitionSpec as P

MESH = pl.DeviceIdType.MESH
BF = jnp.bfloat16
F32 = jnp.float32

S_X0, S_W, S_FZ, S_CA, S_XA, S_GA, S_MA, S_HA, S_TG, S_OB = range(10)
S_AX, S_AY, S_AR, S_CF, S_CD, S_RR, S_RY, S_RX, S_FS = 10, 14, 18, 22, 26, 34, 42, 50, 58
S_FY, S_HB, S_OC, N_SEM = 66, 67, 68, 69
ACROSS_FIRST = ()
ORDER = (
    "o4", "f4", "o5", "f5", "i4", "o6", "f6", "i5", "r4", "o7", "f7", "i6", "r5", "M0",
    "i7", "r6", "g4", "G0", "o3", "b3", "i3", "r7", "g5", "o2", "b2", "i2", "r3", "g6",
    "e4", "e5", "o1", "b1", "i1", "r2", "g7", "H0", "o0", "b0", "i0", "e6", "e7", "r1",
    "H1", "g3", "r0", "T0", "g2", "e3", "g1", "e2", "I0", "g0", "e1", "I1", "e0",
)


def pair(q, d):
    return (q // d) * (2 * d) + q % d


def wide(a, b):
    return jnp.concatenate([a, b], axis=1)


def kernel(
    tok, fac, cot, mixed, tgrad, fgrad,
    xo, xt, go, gt, w, wt, csend, crecv, part, rel, rsum, got, mid, other, xin, acc, fin, hs, hr, ob,
    rsem, ssem,
):
    dp, t = lax.axis_index("dp"), lax.axis_index("tensor")
    c, s = dp % 2, dp // 2
    oc = 1 - c
    xl, y = s // 4, s % 4

    def far(k):
        return (t + 8 + ((k + 1) // 2) * (1 - 2 * (k % 2))) % 16

    def along(i):
        return (y + i) % 4

    def send(src, dst, slot, device):
        pltpu.make_async_remote_copy(
            src_ref=src, dst_ref=dst, send_sem=ssem.at[slot], recv_sem=rsem.at[slot],
            device_id=device, device_id_type=MESH,
        ).start()

    def local(src, dst, slot):
        pltpu.make_async_copy(src, dst, rsem.at[slot]).start()

    def arrived(ref, slot):
        pltpu.make_async_copy(ref, ref, rsem.at[slot]).wait()

    def left(ref, slot):
        pltpu.make_async_copy(ref, ref, ssem.at[slot]).wait()

    def loop(n, body, unroll=1):
        def step(i, carry):
            body(i)
            return carry

        lax.fori_loop(0, n, step, 0, unroll=unroll)

    sibling = (s * 2 + oc, t)
    across = ((s + 4) % 8 * 2 + c, t)

    def to_tensor(src, dst, slot):
        loop(15, lambda k: send(src(far(k)), dst, slot, (dp, far(k))))
        local(src(t), dst, slot)

    def span(level):
        return 4 if level in ACROSS_FIRST else 8

    up, down = along(1), along(3)
    above = ((xl * 4 + up) * 2 + c, t)
    below = ((xl * 4 + down) * 2 + c, t)

    barrier = pltpu.get_barrier_semaphore()

    def greet(device):
        pl.semaphore_signal(barrier, inc=1, device_id=device, device_id_type=MESH)

    loop(15, lambda k: greet((dp, far(k))))
    greet(above)
    greet(below)
    greet(across)
    greet(sibling)
    loop(16, lambda j: local(tok.at[:, pl.ds(pl.multiple_of(j * 128, 128), 128)], xo.at[0, j], S_X0))
    local(fac.at[pl.ds(0, 4)], w, S_W)

    pl.semaphore_wait(barrier, 19)

    rows = pl.ds(pl.multiple_of(s * 16, 16), 16)

    to_tensor(lambda j: fac.at[7, j, c, rows, :], wt.at[3, c, xl, y, t], S_FZ)
    to_tensor(lambda j: fac.at[pl.ds(4, 3), j, c, rows, :], wt.at[pl.ds(0, 3), c, xl, y, t], S_FY)
    to_tensor(
        lambda j: cot.at[:, pl.ds(pl.multiple_of(j * 128, 128), 128)], gt.at[4, t], S_CA
    )

    def weights_low(level):
        return lambda b, k: w[level, b, k]

    def weights_high(lv):
        return lambda b, k: wt[lv, k, :, :, b].reshape(128, 128)

    def matrix(weights, b0, b1):
        return jnp.concatenate(
            [wide(weights(b0, 0), weights(b1, 1)), wide(weights(b0, 1), weights(b1, 0))], axis=0
        )

    def forward(x, at, d, weights):
        def body(q):
            b0 = pair(q, d)
            b1 = b0 + d
            new = jnp.dot(
                wide(x[at, b0], x[at, b1]), matrix(weights, b0, b1), preferred_element_type=F32
            ).astype(BF)
            x[at + 1, b0] = new[:, :128]
            x[at + 1, b1] = new[:, 128:]

        loop(8, body, 8)

    def backward(g, at, d, weights):
        def body(q):
            b0 = pair(q, d)
            b1 = b0 + d
            new = lax.dot_general(
                wide(g[at + 1, b0], g[at + 1, b1]), matrix(weights, b0, b1),
                (((1,), (1,)), ((), ())), preferred_element_type=F32,
            ).astype(BF)
            g[at, b0] = new[:, :128]
            g[at, b1] = new[:, 128:]

        loop(8, body, 8)

    def gradient(x, g, at, d, core, put):
        dl = min(d, 4)

        def body(q):
            b0 = pair(core * 4 + q, d)
            b1 = b0 + d
            dm = lax.dot_general(
                wide(x[at, b0], x[at, b1]), wide(g[at + 1, b0], g[at + 1, b1]),
                (((0,), (0,)), ((), ())), preferred_element_type=F32,
            )
            m0 = pair(q, dl)
            m1 = m0 + dl
            put(m0, 0, dm[:128, :128].reshape(2, 4, 16, 128))
            put(m0, 1, dm[128:, :128].reshape(2, 4, 16, 128))
            put(m1, 1, dm[:128, 128:].reshape(2, 4, 16, 128))
            put(m1, 0, dm[128:, 128:].reshape(2, 4, 16, 128))

        loop(4, body, 4)

    def side(level):
        return (xo, go, level) if level < 4 else (xt, gt, level - 4)

    def grad_out(level):
        x, g, at = side(level)

        def put(m, k, value):
            csend[level, :, :, m, k] = value.astype(BF)

        gradient(x, g, at, 2**at, oc, put)
        send(csend.at[level], crecv.at[level], S_CD + level, sibling)

    def grad_in(level):
        x, g, at = side(level)
        arrived(crecv.at[level], S_CD + level)

        def put(m, k, value):
            part[level, :, :, m, k] = (value + crecv[level, :, :, m, k].astype(F32)).astype(BF)

        gradient(x, g, at, 2**at, c, put)
        if level in ACROSS_FIRST:
            send(part.at[level, 1 - xl], xin.at[level], S_RX + level, across)
        else:
            set_off(level)

    def ways(level):
        return ((xl, 0), (xl, 4)) if level in ACROSS_FIRST else ((0, 0), (1, 0))

    def set_off(level):
        n = span(level)
        (us, um), (ds, dm) = ways(level)
        head = pl.ds(0, n)

        def piece(side_of, way, first):
            return part.at[level, side_of, way, pl.ds(first, n)]

        send(piece(us, along(2), um), rel.at[level, 0, head], S_RR + level, above)
        send(piece(ds, along(2), dm), rel.at[level, 1, head], S_RR + level, below)
        send(piece(ds, up, dm), got.at[level, 1, 0, head], S_RY + level, above)
        send(piece(us, down, um), got.at[level, 0, 0, head], S_RY + level, below)

    def meet(level):
        if level not in ACROSS_FIRST:
            return
        arrived(xin.at[level], S_RX + level)

        def body(m):
            for i in range(4):
                value = part[level, xl, i, m].astype(F32) + xin[level, i, m].astype(F32)
                part[level, xl, i, m] = value.astype(BF)

        loop(8, body, 4)
        set_off(level)

    def relay(level):
        n = span(level)
        (us, um), (ds, dm) = ways(level)
        head = pl.ds(0, n)
        arrived(rel.at[level, :, head], S_RR + level)

        def body(m):
            first = rel[level, 0, m].astype(F32) + part[level, us, up, um + m].astype(F32)
            second = rel[level, 1, m].astype(F32) + part[level, ds, down, dm + m].astype(F32)
            rsum[level, 0, m] = first.astype(BF)
            rsum[level, 1, m] = second.astype(BF)

        loop(n, body, 4)
        send(rsum.at[level, 0, head], got.at[level, 0, 1, head], S_RY + level, above)
        send(rsum.at[level, 1, head], got.at[level, 1, 1, head], S_RY + level, below)

    def gather(level):
        n = span(level)
        arrived(got.at[level, :, :, pl.ds(0, n)], S_RY + level)

        def total(side_of, half, first, m):
            value = part[level, side_of, y, first + m].astype(F32)
            for i in range(2):
                value = value + got[level, half, i, m].astype(F32)
            return value

        if level in ACROSS_FIRST:

            def both(m):
                acc[level, m] = total(xl, 0, 0, m)
                acc[level, 4 + m] = total(xl, 1, 4, m)

            loop(4, both, 4)
            return

        def give(m):
            mid[level, m] = total(1 - xl, 1 - xl, 0, m).astype(BF)

        def keep(m):
            acc[level, m] = total(xl, xl, 0, m)

        loop(8, give, 4)
        send(mid.at[level], other.at[level], S_RX + level, across)
        loop(8, keep, 4)

    def finish(level, out, at):
        if level not in ACROSS_FIRST:
            arrived(other.at[level], S_RX + level)

            def body(m):
                acc[level, m] = acc[level, m] + other[level, m].astype(F32)

            loop(8, body, 4)
        for u in range(2):
            first = 8 * c + 4 * u if level % 4 < 3 else 8 * u + 4 * c
            dst = out.at[at, pl.ds(first, 4)]
            mine = pl.ds(pl.multiple_of(c * 8, 8), 8)
            theirs = pl.ds(pl.multiple_of(oc * 8, 8), 8)
            local(acc.at[level, pl.ds(4 * u, 4), :, mine], dst, S_FS + level)
            send(acc.at[level, pl.ds(4 * u, 4), :, theirs], dst, S_FS + level, sibling)

    arrived(xo.at[0], S_X0)
    arrived(w, S_W)
    for level in range(4):
        forward(xo, level, 2**level, weights_low(level))

    to_tensor(lambda j: xo.at[4, j], xt.at[0, t], S_XA)

    def share(lv):
        piece = wt.at[lv, c, xl, y]
        send(piece, piece, S_AX + lv, across)
        send(piece, piece, S_AY + lv, above)
        send(piece, piece, S_AY + lv, below)

    def share_more(lv):
        piece = wt.at[lv, c, 1 - xl, y]
        arrived(piece, S_AX + lv)
        send(piece, piece, S_AY + lv, above)
        send(piece, piece, S_AY + lv, below)

    def share_on(lv):
        arrived(wt.at[lv, c, :, pl.ds(0, 2)], S_AY + lv)
        first, second = wt.at[lv, c, 0, down], wt.at[lv, c, 1, up]
        send(first, first, S_AR + lv, above)
        send(second, second, S_AR + lv, below)

    def pass_on(lv):
        arrived(wt.at[lv, c, :, 0], S_AR + lv)
        send(wt.at[lv, c], wt.at[lv, c], S_CF + lv, sibling)

    arrived(wt.at[0, c, xl, y], S_FZ)
    share(3)
    arrived(wt.at[pl.ds(0, 3), c, xl, y], S_FY)
    share(2)
    share_more(3)
    share(1)
    share(0)
    share_more(2)
    share_on(3)
    share_more(1)
    share_more(0)
    share_on(2)
    pass_on(3)
    arrived(gt.at[4], S_CA)
    for lv in (3, 2, 1, 0):
        if lv > 1:
            share_on(lv - 2)
        if lv > 0:
            pass_on(lv - 1)
        arrived(wt.at[lv, oc], S_CF + lv)
        backward(gt, lv, 2**lv, weights_high(lv))
    to_tensor(lambda j: gt.at[0, j], go.at[4, t], S_GA)

    def forth(level):
        forward(xt, level - 4, 2 ** (level - 4), weights_high(level - 4))

    def back(level):
        backward(go, level, 2**level, weights_low(level))

    def end(level):
        finish(level, *((fgrad, level) if level < 4 else (fin, level - 4)))

    def mix_out(_):
        own = pl.ds(pl.multiple_of(t * 128, 128), 128)
        to_tensor(lambda j: xt.at[4, j], mixed.at[:, own], S_MA)

    def grad_home(_):
        arrived(go.at[4], S_GA)

    def token_out(_):
        loop(16, lambda j: local(go.at[0, j], tgrad.at[:, pl.ds(pl.multiple_of(j * 128, 128), 128)], S_TG))

    def high_out(g):
        for lv in (2 * g, 2 * g + 1):
            arrived(fin.at[lv], S_FS + 4 + lv)

        def pack(h):
            for lv in (2 * g, 2 * g + 1):
                hs[h, lv] = fin[lv, h].reshape(16, 128).astype(BF)

        loop(16, pack, 4)
        two = pl.ds(2 * g, 2)
        to_tensor(lambda j: hs.at[j, two], hr.at[t, two], (S_HA, S_HB)[g])

    def high_in(g):
        two = pl.ds(2 * g, 2)
        arrived(hr.at[:, two], (S_HA, S_HB)[g])

        def unpack(j):
            for lv in (2 * g, 2 * g + 1):
                ob[lv, j] = hr[j, lv].astype(F32).reshape(2, 8, 128)

        loop(16, unpack, 4)
        local(ob.at[two], fgrad.at[pl.ds(4 + 2 * g, 2)], (S_OB, S_OC)[g])

    steps = dict(
        o=grad_out, i=grad_in, f=forth, b=back, r=relay, g=gather, m=meet, e=end,
        M=mix_out, G=grad_home, T=token_out, H=high_out, I=high_in,
    )
    arrived(xt.at[0], S_XA)
    for step in ORDER:
        steps[step[0]](int(step[1]))

    for level in range(4):
        arrived(fgrad.at[level], S_FS + level)
    arrived(mixed, S_MA)
    arrived(tgrad, S_TG)
    arrived(fgrad.at[pl.ds(4, 2)], S_OB)
    arrived(fgrad.at[pl.ds(6, 2)], S_OC)
    blocks = xo.at[0, pl.ds(0, 15)]
    for slot in (S_CA, S_XA, S_GA, S_MA):
        left(blocks, slot)
    left(hs.at[pl.ds(0, 15), 0], S_FZ)
    left(hs.at[pl.ds(0, 15), pl.ds(0, 3)], S_FY)
    left(hs.at[pl.ds(0, 15), pl.ds(0, 2)], S_HA)
    left(hs.at[pl.ds(0, 15), pl.ds(0, 2)], S_HB)
    for lv in range(4):
        left(wt.at[lv, 0, 0, 0], S_AX + lv)
        left(wt.at[lv, 0, :, pl.ds(0, 2)], S_AY + lv)
        left(wt.at[lv, 0, :, 0], S_AR + lv)
        left(wt.at[lv, 0], S_CF + lv)
    for level in range(8):
        left(csend.at[level], S_CD + level)
        left(rel.at[level, :, pl.ds(0, span(level))], S_RR + level)
        left(got.at[level, :, :, pl.ds(0, span(level))], S_RY + level)
        left(part.at[level, 0] if level in ACROSS_FIRST else mid.at[level], S_RX + level)
        left(acc.at[level, :, :, pl.ds(0, 8)], S_FS + level)


def hand_over(a, b, c, a_out, b_out, c_out, a_held, b_held, c_held, sem):
    moves = ((c, c_held, c_out), (a, a_held, a_out), (b, b_held, b_out))
    into = [pltpu.make_async_copy(m[0], m[1], sem.at[i]) for i, m in enumerate(moves)]
    out = [pltpu.make_async_copy(m[1], m[2], sem.at[3 + i]) for i, m in enumerate(moves)]
    for copy in into:
        copy.start()
    for i in range(3):
        into[i].wait()
        out[i].start()
    for copy in out:
        copy.wait()


def per_device(tokens, factors, cotangent):
    hbm = pl.BlockSpec(memory_space=pl.ANY)
    acts = pltpu.VMEM((5, 16, 128, 128), BF)
    grads = pltpu.VMEM((8, 2, 4, 8, 2, 16, 128), BF)
    slab = pltpu.VMEM((8, 8, 2, 16, 128), BF)
    two = pltpu.VMEM((8, 2, 8, 2, 16, 128), BF)
    shapes = (
        jax.ShapeDtypeStruct((128, 2048), BF),
        jax.ShapeDtypeStruct((128, 2048), BF),
        jax.ShapeDtypeStruct((8, 16, 2, 8, 128), F32),
    )
    results = pl.pallas_call(
        kernel,
        out_shape=shapes,
        in_specs=[hbm] * 3,
        out_specs=[hbm] * 3,
        scratch_shapes=[
            acts, acts, acts, acts,
            pltpu.VMEM((4, 16, 2, 128, 128), BF),
            pltpu.VMEM((4, 2, 2, 4, 16, 16, 128), BF),
            grads, grads, grads, two, two, pltpu.VMEM((8, 2, 2, 8, 2, 16, 128), BF), slab, slab,
            pltpu.VMEM((2, 4, 8, 2, 16, 128), BF),
            pltpu.VMEM((8, 8, 2, 16, 128), F32),
            pltpu.VMEM((4, 16, 2, 8, 128), F32),
            pltpu.VMEM((16, 4, 16, 128), BF),
            pltpu.VMEM((16, 4, 16, 128), BF),
            pltpu.VMEM((4, 16, 2, 8, 128), F32),
            pltpu.SemaphoreType.DMA((N_SEM,)),
            pltpu.SemaphoreType.DMA((N_SEM,)),
        ],
        compiler_params=pltpu.CompilerParams(
            collective_id=0, has_side_effects=True, vmem_limit_bytes=56 * 1024 * 1024
        ),
        cost_estimate=pl.CostEstimate(flops=3221225472, bytes_accessed=12582912, transcendentals=0),
        name="butterfly",
    )(tokens, factors, cotangent)
    return pl.pallas_call(
        hand_over,
        out_shape=shapes,
        in_specs=[hbm] * 3,
        out_specs=[hbm] * 3,
        scratch_shapes=[pltpu.VMEM(x.shape, x.dtype) for x in shapes] + [pltpu.SemaphoreType.DMA((6,))],
        name="hand_over",
    )(*results)


def solution(mesh):
    placed = (P("dp", "tensor"), P(None, "tensor", None, None, None), P("dp", "tensor"))
    return jax.shard_map(
        per_device,
        mesh=mesh,
        in_specs=placed,
        out_specs=(P("dp", "tensor"), P("dp", "tensor"), P(None, "tensor", None, "dp", None)),
        check_vma=False,
    )
```
